32 devices in a mesh: grp: 2 (over y), blk: 4 (over z), rep: 2 (over x), sub: 2 (over core).
Axes of the slice: x: 2, y: 2, z: 4, core: 2. Of those that a mesh axis runs over, the one named last changes fastest.
Arguments:
- image_feature_vectors: float32 [16384, 768], P(('grp', 'blk', 'rep', 'sub')), parts along dimension 0
- centroid_group_label: int32 [16384], P(('grp', 'blk', 'rep', 'sub')), parts along dimension 0, may hold values from 0 to 23, as said below
- group_member_sizes: int32 [48], P('grp'), parts along dimension 0, may hold values from 32 to 512, as said below
- softmax_heat_factors: float32 [48], P('grp'), parts along dimension 0, may hold values from 0.1 to 1
Outputs:
- scores: float32 [16384], P(('grp', 'blk', 'rep', 'sub')), parts along dimension 0
The draws below stay inside these ranges and needn't reach their ends.
There are 2 independent parts, one for each index of `grp`. The reference program is written for one: setup_inputs(seed, part) draws one part's arguments, and reference() takes and returns one part's arrays. A program takes and returns all parts, laid end to end along the dimension named above; each array names one. Nothing has to cross between parts.
Inputs may be any that keep to these rules, and one draw needn't show every extreme that they name: `centroid_group_label`: cluster c belongs to owner c // 3, owners being numbered over (blk, rep) with blk slowest. The rows of cluster c number exactly group_member_sizes[c]. Every owner's clusters hold 1024 rows together. Each device holds at most 96 rows of the clusters of one owner, exactly 96 for some owner; the devices that share one sub index hold exactly 512 rows of each owner's clusters together. `group_member_sizes`: one cluster of every owner holds exactly 512 rows.
All inputs are finite; a program needn't handle non-finite values.
Results may differ from the reference program's by a relative error of at most 0.0003.
Values may be sent and summed in bfloat16 or wider, within the bound.
A program may use at most 64 MiB of HBM per device.

```python
import math
import jax
import jax.numpy as jnp
from jax import lax

D = 768
ROW_DEV = 512
GROUPS_EACH_PEER = 3
OWN_ROWS = 1024
MOST = 512
LEAST = 32
GROUP_TOTAL = 24
N_BLK = 4
N_REP = 2
N_SUB = 2


family_count = 16


def shuffle_last(subkey, values):
    length = values.shape[-1]
    ranking = jax.random.randint(subkey, values.shape, 0, 1 << 18) * length + jnp.arange(length, dtype=jnp.int32)
    sorted_order = jnp.argsort(ranking, axis=-1)
    return jnp.take_along_axis(values, sorted_order, axis=-1)


def rank_equal(labels):
    length = labels.shape[-1]
    sorted_order = jnp.argsort(labels, axis=-1, stable=True)
    ordered = jnp.take_along_axis(labels, sorted_order, axis=-1)
    first_same = jax.vmap(lambda values: jnp.searchsorted(values, values, side='left'))(ordered)
    ranked = jnp.arange(length, dtype=jnp.int32)[None, :] - first_same.astype(jnp.int32)
    row_index = jnp.arange(labels.shape[0], dtype=jnp.int32)[:, None]
    return jnp.zeros(labels.shape, jnp.int32).at[row_index, sorted_order].set(ranked)


def layout(base_key):
    owners = N_BLK * N_REP
    devices = owners * N_SUB
    share_rows = ROW_DEV // owners
    spread = share_rows // 2
    subkeys = jax.random.split(base_key, 6)
    extra_rows = OWN_ROWS - MOST - (GROUPS_EACH_PEER - 1) * LEAST
    cut_points = jnp.sort(jax.random.randint(subkeys[0], (owners, GROUPS_EACH_PEER - 2), 0, extra_rows + 1), axis=1)
    bounds = jnp.concatenate([jnp.zeros((owners, 1), jnp.int32), cut_points, jnp.full((owners, 1), extra_rows, jnp.int32)], axis=1)
    pieces = jnp.diff(bounds, axis=1) + LEAST
    entries = jnp.concatenate([jnp.full((owners, 1), MOST, jnp.int32), pieces], axis=1)
    lengths = shuffle_last(subkeys[1], entries)
    offsets_cycle = jax.random.randint(subkeys[2], (N_SUB, owners), 0, spread + 1)
    offsets_cycle = offsets_cycle.at[:, 0].set(spread).at[:, 1].set(0)
    rotation = shuffle_last(subkeys[3], jnp.broadcast_to(jnp.arange(owners, dtype=jnp.int32), (N_SUB, owners)))
    source = jnp.arange(owners, dtype=jnp.int32)[:, None, None]
    position_index = (rotation[None, :, :] + source) % owners
    next_index = (position_index + 1) % owners
    cycle_wide = jnp.broadcast_to(offsets_cycle[None, :, :], (owners, N_SUB, owners))
    counts = share_rows + jnp.take_along_axis(cycle_wide, position_index, axis=2) - jnp.take_along_axis(cycle_wide, next_index, axis=2)
    counts = counts.reshape(devices, owners)
    cumulative = jnp.cumsum(counts, axis=1)
    position = jnp.arange(ROW_DEV, dtype=jnp.int32)
    sorted_owner = jax.vmap(lambda bounds_row: jnp.searchsorted(bounds_row, position, side='right'))(cumulative).astype(jnp.int32)
    row_owner = shuffle_last(subkeys[4], sorted_owner)
    local_rank = rank_equal(row_owner)
    before_dev = jnp.cumsum(counts, axis=0) - counts
    first_rank = jnp.take_along_axis(before_dev, row_owner, axis=1)
    global_rank = first_rank + local_rank
    size_bounds = jnp.cumsum(lengths, axis=1)
    member = jnp.arange(OWN_ROWS, dtype=jnp.int32)
    label_sorted = jax.vmap(lambda bounds_row: jnp.searchsorted(bounds_row, member, side='right'))(size_bounds).astype(jnp.int32)
    labels = shuffle_last(subkeys[5], label_sorted)
    picked = labels[row_owner, global_rank]
    cluster_of = (row_owner * GROUPS_EACH_PEER + picked).reshape(devices * ROW_DEV)
    return (lengths.reshape(owners * GROUPS_EACH_PEER), cluster_of)


def draw_centroid_group_label(key, part):
    lengths, cluster_of = layout(key)
    return cluster_of


def draw_group_member_sizes(key, part):
    lengths, cluster_of = layout(key)
    return lengths


def draw_image_feature_vectors(key, part):
    lengths, cluster_of = layout(key)
    key = jax.random.fold_in(key, 7)
    subkeys = jax.random.split(key, 9)
    length = cluster_of.shape[0]
    clusters = GROUPS_EACH_PEER * N_BLK * N_REP
    centers = jax.random.normal(subkeys[0], (clusters, D), jnp.float32)
    family_strength = jax.random.uniform(subkeys[1], (clusters * family_count, 1), jnp.float32, 0.0, 3.0)
    family_of = cluster_of * family_count + jax.random.randint(subkeys[5], (length,), 0, family_count)
    family_noise = jax.random.normal(subkeys[6], (clusters * family_count, D), jnp.float32)
    tight = jax.random.randint(subkeys[7], (length, 1), 0, 3) == 0
    loose_weight = jax.random.uniform(subkeys[8], (length, 1), jnp.float32, 0.0, 1.0)
    family_weight = jnp.where(tight, 1.0, loose_weight)
    fresh_weight = jnp.where(tight, 0.14, 1.0)
    shared = family_strength[family_of] * centers[cluster_of] + family_weight * family_noise[family_of]
    noise = jax.random.normal(subkeys[2], (length, D), jnp.float32)
    return shared + fresh_weight * noise


def setup_inputs(seed: int = 0, part: int = 0) -> dict:
    seeds = jax.random.split(jax.random.key(seed), 5)
    part_keys = jax.random.split(jax.random.fold_in(seeds[4], part), 5)
    image_feature_vectors = draw_image_feature_vectors(jax.random.fold_in(jax.random.fold_in(seeds[4], part), 71), part)
    centroid_group_label = draw_centroid_group_label(jax.random.fold_in(jax.random.fold_in(seeds[4], part), 71), part)
    group_member_sizes = draw_group_member_sizes(jax.random.fold_in(jax.random.fold_in(seeds[4], part), 71), part)
    softmax_heat_factors = jnp.clip(jnp.exp(jax.random.uniform(part_keys[3], (GROUP_TOTAL,), jnp.float32, math.log(0.1), math.log(1.0))), 0.1, 1.0)
    return {"image_feature_vectors": image_feature_vectors, "centroid_group_label": centroid_group_label, "group_member_sizes": group_member_sizes, "softmax_heat_factors": softmax_heat_factors}


def normalize_rows(image_feature_vectors):
    squares = lax.optimization_barrier(jnp.sum(image_feature_vectors * image_feature_vectors, axis=1, keepdims=True))
    return (image_feature_vectors * lax.rsqrt(squares + 1e-06)).astype(jnp.bfloat16)

def reference(image_feature_vectors, centroid_group_label, group_member_sizes, softmax_heat_factors):
    owners = N_BLK * N_REP
    unit_vecs = normalize_rows(image_feature_vectors)
    sorted_order = jnp.argsort(centroid_group_label, stable=True)
    grouped = unit_vecs[sorted_order].reshape(owners, OWN_ROWS, D)
    labels = centroid_group_label[sorted_order].reshape(owners, OWN_ROWS)
    undo_shuffle_mapping = 1.0 / softmax_heat_factors
    log_sizes = jnp.log(group_member_sizes.astype(jnp.float32))

    def one_owner(owner_pair):
        members, member_labels = owner_pair
        wide_rows = members.astype(jnp.float32)
        cosine = jnp.dot(wide_rows, wide_rows.T, precision=lax.Precision.HIGHEST, preferred_element_type=jnp.float32)
        same_cluster = member_labels[:, None] == member_labels[None, :]
        row_scale = undo_shuffle_mapping[member_labels]
        weight = jnp.where(same_cluster, jnp.exp((cosine - 1.0) * row_scale[:, None]), 0.0)
        total = lax.optimization_barrier(jnp.sum(weight, axis=1))
        return row_scale + jnp.log(total) - log_sizes[member_labels]
    flat_scores = lax.map(one_owner, (grouped, labels)).reshape(-1)
    return jnp.zeros(flat_scores.shape, jnp.float32).at[sorted_order].set(flat_scores)
```

```python
import functools

import jax
import jax.numpy as jnp
from jax import lax
from jax.experimental import pallas as pl
from jax.experimental.pallas import tpu as pltpu
from jax.sharding import PartitionSpec as P

D = 768
GROUPS_EACH_PEER = 3
MESH = pl.DeviceIdType.MESH
F32 = jnp.float32
BF16 = jnp.bfloat16


def kernel(
    n_blk, n_rep, n_sub, slots,
    x_ref, label_ref, sizes_ref, heats_ref, out_ref,
    unit, out_rows, out_tags, rows, tags, back_out, back_in,
    row_send, row_recv, tag_send, tag_recv, fwd_send, fwd_recv,
    fwd_tag_send, fwd_tag_recv, back_send, back_recv,
):
    owners = n_blk * n_rep
    count = x_ref.shape[0]
    me = lax.axis_index("blk") * n_rep + lax.axis_index("rep")
    sub = lax.axis_index("sub")

    def device(owner):
        return {"blk": owner // n_rep, "rep": owner % n_rep}

    sibling = {"sub": 1 - sub}

    def peers(body):
        def step(k, carry):
            body(k, lax.rem(me + k, owners))
            return carry

        lax.fori_loop(1, owners, step, 0, unroll=owners <= 16)

    barrier = pltpu.get_barrier_semaphore()
    peers(lambda k, o: pl.semaphore_signal(barrier, inc=1, device_id=device(o), device_id_type=MESH))
    pl.semaphore_signal(barrier, inc=1, device_id=sibling, device_id_type=MESH)

    labels = label_ref[...]
    owner_range = lax.broadcasted_iota(jnp.int32, (owners, count), 0) * GROUPS_EACH_PEER
    local = labels - owner_range
    mine_owner = (local >= 0) & (local < GROUPS_EACH_PEER)
    upper = (
        lax.broadcasted_iota(jnp.int32, (count, count), 0)
        < lax.broadcasted_iota(jnp.int32, (count, count), 1)
    )
    before = jnp.dot(
        jnp.where(mine_owner, 1.0, 0.0).astype(BF16),
        jnp.where(upper, 1.0, 0.0).astype(BF16),
        preferred_element_type=F32,
    )
    rank = jnp.sum(jnp.where(mine_owner, before, 0.0), axis=0, keepdims=True).astype(jnp.int32)
    first = jnp.sum(jnp.where(mine_owner, owner_range, 0), axis=0, keepdims=True)
    member = labels - first
    code = first * 256 + rank
    slot_range = lax.broadcasted_iota(jnp.int32, (slots, count), 0)
    wide_range = lax.broadcasted_iota(jnp.int32, (128, count), 0)
    member_hot = jnp.where(
        lax.broadcasted_iota(jnp.int32, (8, count), 0) == member, 1.0, 0.0
    ).astype(BF16)

    def picked(owner, span):
        return jnp.where(span + owner * (GROUPS_EACH_PEER * 256) == code, 1.0, 0.0).astype(BF16)

    def tags_for(owner):
        return lax.dot_general(
            member_hot, picked(owner, wide_range), (((1,), (1,)), ((), ())),
            preferred_element_type=F32,
        )

    def rows_for(owner):
        return jnp.dot(
            picked(owner, slot_range), unit[...], preferred_element_type=F32
        ).astype(BF16)

    x = x_ref[...]
    squares = jnp.sum(x * x, axis=1, keepdims=True)
    unit[...] = (x * lax.rsqrt(squares + 1e-06)).astype(BF16)

    pl.semaphore_wait(barrier, owners)

    def row_copy(o, slot):
        return pltpu.make_async_remote_copy(
            src_ref=out_rows.at[o], dst_ref=rows.at[0, slot],
            send_sem=row_send.at[o], recv_sem=row_recv.at[slot],
            device_id=device(o), device_id_type=MESH,
        )

    def tag_copy(o, slot):
        return pltpu.make_async_remote_copy(
            src_ref=out_tags.at[o], dst_ref=tags.at[0, slot],
            send_sem=tag_send.at[o], recv_sem=tag_recv.at[slot],
            device_id=device(o), device_id_type=MESH,
        )

    def back_copy(o, slot):
        return pltpu.make_async_remote_copy(
            src_ref=back_out.at[o], dst_ref=back_in.at[slot],
            send_sem=back_send.at[o], recv_sem=back_recv.at[slot],
            device_id=device(o), device_id_type=MESH,
        )

    def forward(o):
        return pltpu.make_async_remote_copy(
            src_ref=rows.at[0, o], dst_ref=rows.at[1, o],
            send_sem=fwd_send.at[o], recv_sem=fwd_recv.at[o],
            device_id=sibling, device_id_type=MESH,
        )

    def send(k, o):
        out_tags[o] = tags_for(o)
        tag_copy(o, me).start()
        out_rows[o] = rows_for(o)
        row_copy(o, me).start()

    peers(send)
    tags[0, me] = tags_for(me)
    rows[0, me] = rows_for(me)
    forward(me).start()

    def source(k):
        return lax.rem(me - k + owners, owners)

    def arrive(k, o):
        o = source(k)
        row_copy(o, o).wait_recv()
        forward(o).start()

    def arrive_tag(k, o):
        o = source(k)
        tag_copy(o, o).wait_recv()

    peers(arrive_tag)
    forward_tags = pltpu.make_async_remote_copy(
        src_ref=tags.at[0], dst_ref=tags.at[1],
        send_sem=fwd_tag_send, recv_sem=fwd_tag_recv,
        device_id=sibling, device_id_type=MESH,
    )
    forward_tags.start()

    hot = jnp.concatenate([tags[0, o][:, :slots] for o in range(owners)], axis=1)
    heat = jnp.zeros_like(hot[0:1])
    size = jnp.zeros_like(heat)
    for g in range(GROUPS_EACH_PEER):
        at = me * GROUPS_EACH_PEER + g
        heat = heat + hot[g : g + 1] * heats_ref[at]
        size = jnp.where(hot[g : g + 1] > 0.5, sizes_ref[at].astype(F32), size)
    valid = heat > 0.0
    inverse = 1.0 / jnp.where(valid, heat, 1.0)
    offset = inverse - jnp.log(jnp.where(valid, size, 1.0))
    hot = hot.astype(BF16)

    peers(arrive)
    forward_tags.wait_recv()

    own = rows[0].reshape(owners * slots, D)

    def column(s, o):
        cosine = lax.dot_general(
            rows[s, o], own, (((1,), (1,)), ((), ())), preferred_element_type=F32
        )
        same = lax.dot_general(
            tags[s, o][:, :slots].astype(BF16), hot, (((0,), (0,)), ((), ())),
            preferred_element_type=F32,
        )
        weight = jnp.exp((cosine - 1.0) * inverse) * same
        return jnp.sum(weight, axis=0, keepdims=True)

    total = jnp.zeros((1, owners * slots), F32)
    total = lax.fori_loop(0, owners, lambda o, t: t + column(0, o), total)

    def other(k, t):
        o = lax.rem(1 * me + k, owners)
        forward(o).wait_recv()
        return t + column(1, o)

    total = lax.fori_loop(0, owners, other, total)
    scores = jnp.where(valid, offset + jnp.log(jnp.where(valid, total, 1.0)), 0.0)
    for o in range(owners):
        back_out[o] = jnp.zeros((8, 128), F32)
        back_out[o, 0:1, 0:slots] = scores[:, o * slots : (o + 1) * slots]
    back_in[me] = back_out[me]

    peers(lambda k, o: back_copy(o, me).start())

    def drain(k, o):
        tag_copy(o, me).wait_send()
        row_copy(o, me).wait_send()
        forward(o).wait_send()

    peers(drain)
    forward(me).wait_send()
    forward_tags.wait_send()

    def arrive_back(k, o):
        back_copy(source(k), source(k)).wait_recv()

    peers(arrive_back)
    table = back_in[:, 0, :]
    spread = jnp.where(wide_range == rank, 1.0, 0.0)
    found = jnp.dot(table, spread, precision=lax.Precision.HIGHEST, preferred_element_type=F32)
    out_ref[...] = jnp.sum(jnp.where(mine_owner, found, 0.0), axis=0, keepdims=True)
    peers(lambda k, o: back_copy(o, me).wait_send())


def on_device(vectors, labels, sizes, heats):
    count = vectors.shape[0]
    n_blk, n_rep, n_sub = (lax.axis_size(a) for a in ("blk", "rep", "sub"))
    owners = n_blk * n_rep
    share = count // owners
    slots = -(-(share + share // 2) // 16) * 16
    dma = pltpu.SemaphoreType.DMA
    out = pl.pallas_call(
        functools.partial(kernel, n_blk, n_rep, n_sub, slots),
        out_shape=jax.ShapeDtypeStruct((1, count), F32),
        in_specs=[
            pl.BlockSpec(memory_space=pltpu.VMEM),
            pl.BlockSpec(memory_space=pltpu.VMEM),
            pl.BlockSpec(memory_space=pltpu.SMEM),
            pl.BlockSpec(memory_space=pltpu.SMEM),
        ],
        out_specs=pl.BlockSpec(memory_space=pltpu.VMEM),
        scratch_shapes=[
            pltpu.VMEM((count, D), BF16),
            pltpu.VMEM((owners, slots, D), BF16),
            pltpu.VMEM((owners, 8, 128), F32),
            pltpu.VMEM((n_sub, owners, slots, D), BF16),
            pltpu.VMEM((n_sub, owners, 8, 128), F32),
            pltpu.VMEM((owners, 8, 128), F32),
            pltpu.VMEM((owners, 8, 128), F32),
            dma((owners,)), dma((owners,)), dma((owners,)), dma((owners,)),
            dma((owners,)), dma((owners,)), dma, dma,
            dma((owners,)), dma((owners,)),
        ],
        compiler_params=pltpu.CompilerParams(
            collective_id=0, has_side_effects=True, vmem_limit_bytes=48 << 20
        ),
    )(vectors, labels.reshape(1, count), sizes, heats)
    return out.reshape(count)


def solution(mesh):
    placed = (
        P(("grp", "blk", "rep", "sub"), None),
        P(("grp", "blk", "rep", "sub")),
        P("grp"),
        P("grp"),
    )
    return jax.shard_map(
        on_device,
        mesh=mesh,
        in_specs=placed,
        out_specs=P(("grp", "blk", "rep", "sub")),
        check_vma=False,
    )
```

```python
import functools

import jax
import jax.numpy as jnp
from jax import lax
from jax.experimental import pallas as pl
from jax.experimental.pallas import tpu as pltpu
from jax.sharding import PartitionSpec as P

D = 768
GROUPS_EACH_PEER = 3
ORDER = (0, 7, 6, 5, 4, 3, 2, 1)
LOADS = 4
MESH = pl.DeviceIdType.MESH
F32 = jnp.float32
BF16 = jnp.bfloat16


def kernel(
    n_blk, n_rep, n_sub, slots,
    x_hbm, label_ref, sizes_ref, heats_ref, out_ref,
    x_ref, unit, out_rows, out_tags, rows, tags, sums, back_out, back_in,
    load_sem, row_send, row_recv, tag_send, tag_recv, fwd_send, fwd_recv,
    fwd_tag_send, fwd_tag_recv, back_send, back_recv,
):
    owners = n_blk * n_rep
    bits = owners.bit_length() - 1
    parts = min(owners, len(ORDER))
    per = owners // parts
    span = per * slots
    count = x_ref.shape[0]
    me = lax.axis_index("blk") * n_rep + lax.axis_index("rep")
    sibling = {"sub": 1 - lax.axis_index("sub")}
    piece = count // LOADS

    def load(c):
        at = pl.ds(c * piece, piece)
        return pltpu.make_async_copy(x_hbm.at[at], x_ref.at[at], load_sem.at[c])

    for c in range(LOADS):
        load(c).start()

    def peer(k):
        o = 0
        for b in range(bits):
            o = o + lax.rem(lax.rem(me // 2**b, 2) + (k // 2**b) % 2, 2) * 2**b
        return o

    def device(owner):
        return {"blk": owner // n_rep, "rep": lax.rem(owner, n_rep)}

    def each(p, body):
        def step(q, carry):
            body(p * per + q, peer(ORDER[p] * per + q))
            return carry

        first = 1 if p == 0 else 0
        if per == 1:
            if not first:
                step(0, 0)
        else:
            lax.fori_loop(first, per, step, 0)

    def peers(body):
        for p in range(parts):
            each(p, body)

    barrier = pltpu.get_barrier_semaphore()
    peers(lambda n, o: pl.semaphore_signal(barrier, inc=1, device_id=device(o), device_id_type=MESH))
    pl.semaphore_signal(barrier, inc=1, device_id=sibling, device_id_type=MESH)

    labels = label_ref[...]
    owner_range = lax.broadcasted_iota(jnp.int32, (owners, count), 0) * GROUPS_EACH_PEER
    local = labels - owner_range
    mine_owner = (local >= 0) & (local < GROUPS_EACH_PEER)
    upper = (
        lax.broadcasted_iota(jnp.int32, (count, count), 0)
        < lax.broadcasted_iota(jnp.int32, (count, count), 1)
    )
    before = jnp.dot(
        jnp.where(mine_owner, 1.0, 0.0).astype(BF16),
        jnp.where(upper, 1.0, 0.0).astype(BF16),
        preferred_element_type=F32,
    )
    rank = jnp.sum(jnp.where(mine_owner, before, 0.0), axis=0, keepdims=True).astype(jnp.int32)
    first = jnp.sum(jnp.where(mine_owner, owner_range, 0), axis=0, keepdims=True)
    member = labels - first
    code = first * 256 + rank
    slot_range = lax.broadcasted_iota(jnp.int32, (slots, count), 0)
    wide_range = lax.broadcasted_iota(jnp.int32, (128, count), 0)
    tag_range = lax.broadcasted_iota(jnp.int32, (8, count), 0)
    tag_table = jnp.where(
        tag_range == GROUPS_EACH_PEER,
        (member + 1).astype(F32),
        jnp.where(tag_range == member, 1.0, 0.0),
    ).astype(BF16)

    def picked(owner, slot):
        return jnp.where(slot + owner * (GROUPS_EACH_PEER * 256) == code, 1.0, 0.0).astype(BF16)

    def tags_for(owner):
        return lax.dot_general(
            tag_table, picked(owner, wide_range), (((1,), (1,)), ((), ())),
            preferred_element_type=F32,
        )

    def rows_for(owner):
        return jnp.dot(
            picked(owner, slot_range), unit[...], preferred_element_type=F32
        ).astype(BF16)

    def normalise(c):
        load(c).wait()
        x = x_ref[c * piece : (c + 1) * piece]
        squares = jnp.sum(x * x, axis=1, keepdims=True)
        unit[c * piece : (c + 1) * piece] = (x * lax.rsqrt(squares + 1e-06)).astype(BF16)

    for c in range(LOADS):
        normalise(c)

    def row_copy(n, o):
        return pltpu.make_async_remote_copy(
            src_ref=out_rows.at[n], dst_ref=rows.at[0, n],
            send_sem=row_send.at[n], recv_sem=row_recv.at[n],
            device_id=device(o), device_id_type=MESH,
        )

    def tag_copy(n, o):
        return pltpu.make_async_remote_copy(
            src_ref=out_tags.at[n], dst_ref=tags.at[0, n],
            send_sem=tag_send.at[n], recv_sem=tag_recv.at[n],
            device_id=device(o), device_id_type=MESH,
        )

    def back_copy(n, o):
        return pltpu.make_async_remote_copy(
            src_ref=back_out.at[n], dst_ref=back_in.at[n],
            send_sem=back_send.at[n], recv_sem=back_recv.at[n],
            device_id=device(o), device_id_type=MESH,
        )

    def forward(n):
        return pltpu.make_async_remote_copy(
            src_ref=rows.at[0, n], dst_ref=rows.at[1, n],
            send_sem=fwd_send.at[n], recv_sem=fwd_recv.at[n],
            device_id=sibling, device_id_type=MESH,
        )

    def send_tags(n, o):
        out_tags[n] = tags_for(o)
        tag_copy(n, o).start()

    def send_rows(n, o):
        out_rows[n] = rows_for(o)
        row_copy(n, o).start()

    starting = [p for p in range(1, parts)] + [0]
    for turn, p in enumerate(starting):
        if turn == 0 and parts > 1:
            def first_rows(n, o):
                out_rows[n] = rows_for(o)

            each(p, first_rows)
            pl.semaphore_wait(barrier, owners)
            each(p, lambda n, o: row_copy(n, o).start())
            peers(send_tags)
            tags[0, 0] = tags_for(me)
        else:
            each(p, send_rows)
    rows[0, 0] = rows_for(me)
    forward(0).start()

    peers(lambda n, o: tag_copy(n, o).wait_recv())
    forward_tags = pltpu.make_async_remote_copy(
        src_ref=tags.at[0], dst_ref=tags.at[1],
        send_sem=fwd_tag_send, recv_sem=fwd_tag_recv,
        device_id=sibling, device_id_type=MESH,
    )
    forward_tags.start()

    hot = jnp.concatenate([tags[0, n][:, :slots] for n in range(owners)], axis=1)
    heat = jnp.zeros_like(hot[0:1])
    size = jnp.zeros_like(heat)
    for g in range(GROUPS_EACH_PEER):
        at = me * GROUPS_EACH_PEER + g
        heat = heat + hot[g : g + 1] * heats_ref[at]
        size = jnp.where(hot[g : g + 1] > 0.5, sizes_ref[at].astype(F32), size)
    valid = heat > 0.0
    inverse = 1.0 / jnp.where(valid, heat, 1.0)
    offset = inverse - jnp.log(jnp.where(valid, size, 1.0))
    tag_row = hot[GROUPS_EACH_PEER : GROUPS_EACH_PEER + 1]
    forward_tags.wait_recv()

    def tag_column(s, lo, hi):
        return jnp.concatenate(
            [
                tags[s, n].T[:slots, GROUPS_EACH_PEER : GROUPS_EACH_PEER + 1]
                for n in range(lo * per, hi * per)
            ],
            axis=0,
        )

    def block(s, lo, hi):
        return rows[s, lo * per : hi * per].reshape((hi - lo) * span, D)

    def column(s, j0, j1, i0, i1):
        cosine = lax.dot_general(
            block(s, j0, j1), block(0, i0, i1), (((1,), (1,)), ((), ())),
            preferred_element_type=F32,
        )
        at = slice(i0 * span, i1 * span)
        weight = jnp.where(
            tag_column(s, j0, j1) == tag_row[:, at],
            jnp.exp((cosine - 1.0) * inverse[:, at]),
            0.0,
        )
        return jnp.sum(weight, axis=0, keepdims=True)

    def arrive(n, o):
        row_copy(n, o).wait_recv()
        forward(n).start()

    sums[...] = jnp.zeros_like(sums)
    back_out[...] = jnp.zeros_like(back_out)
    late = []
    for p in range(parts):
        each(p, arrive)
        upto = slice(0, (p + 1) * span)
        sums[:, upto] += column(0, p, p + 1, 0, p + 1)
        if p:
            late.append(column(0, 0, p, p, p + 1) + column(1, 0, p, p, p + 1))
        else:
            late.append(jnp.zeros((1, span), F32))
            forward(0).wait_recv()
        each(p, lambda n, o: forward(n).wait_recv())
        sums[:, upto] += column(1, p, p + 1, 0, p + 1)

    total = sums[...] + jnp.concatenate(late, axis=1)
    scores = jnp.where(valid, offset + jnp.log(jnp.where(valid, total, 1.0)), 0.0)
    for n in range(owners):
        back_out[n, 0:1, 0:slots] = scores[:, n * slots : (n + 1) * slots]
    peers(lambda n, o: back_copy(n, o).start())
    back_in[0] = back_out[0]

    def drain(n, o):
        tag_copy(n, o).wait_send()
        row_copy(n, o).wait_send()
        forward(n).wait_send()

    peers(drain)
    forward(0).wait_send()
    forward_tags.wait_send()
    spread = jnp.where(wide_range == rank, 1.0, 0.0)

    peers(lambda n, o: back_copy(n, o).wait_recv())
    table = back_in[:, 0, :]
    found = jnp.dot(table, spread, precision=lax.Precision.HIGHEST, preferred_element_type=F32)
    out = jnp.where(first == me * GROUPS_EACH_PEER, found[0:1], 0.0)
    for n in range(1, owners):
        o = peer(ORDER[n // per] * per + n % per)
        out = jnp.where(first == o * GROUPS_EACH_PEER, found[n : n + 1], out)
    out_ref[...] = out
    peers(lambda n, o: back_copy(n, o).wait_send())


def on_device(vectors, labels, sizes, heats):
    count = vectors.shape[0]
    n_blk, n_rep, n_sub = (lax.axis_size(a) for a in ("blk", "rep", "sub"))
    owners = n_blk * n_rep
    share = count // owners
    slots = -(-(share + share // 2) // 16) * 16
    dma = pltpu.SemaphoreType.DMA
    out = pl.pallas_call(
        functools.partial(kernel, n_blk, n_rep, n_sub, slots),
        out_shape=jax.ShapeDtypeStruct((1, count), F32),
        in_specs=[
            pl.BlockSpec(memory_space=pltpu.HBM),
            pl.BlockSpec(memory_space=pltpu.VMEM),
            pl.BlockSpec(memory_space=pltpu.SMEM),
            pl.BlockSpec(memory_space=pltpu.SMEM),
        ],
        out_specs=pl.BlockSpec(memory_space=pltpu.VMEM),
        scratch_shapes=[
            pltpu.VMEM((count, D), F32),
            pltpu.VMEM((count, D), BF16),
            pltpu.VMEM((owners, slots, D), BF16),
            pltpu.VMEM((owners, 8, 128), F32),
            pltpu.VMEM((n_sub, owners, slots, D), BF16),
            pltpu.VMEM((n_sub, owners, 8, 128), F32),
            pltpu.VMEM((1, owners * slots), F32),
            pltpu.VMEM((owners, 8, 128), F32),
            pltpu.VMEM((owners, 8, 128), F32),
            dma((LOADS,)),
            dma((owners,)), dma((owners,)), dma((owners,)), dma((owners,)),
            dma((owners,)), dma((owners,)), dma, dma,
            dma((owners,)), dma((owners,)),
        ],
        compiler_params=pltpu.CompilerParams(
            collective_id=0, has_side_effects=True, vmem_limit_bytes=48 << 20
        ),
    )(vectors, labels.reshape(1, count), sizes, heats)
    return out.reshape(count)


def solution(mesh):
    placed = (
        P(("grp", "blk", "rep", "sub"), None),
        P(("grp", "blk", "rep", "sub")),
        P("grp"),
        P("grp"),
    )
    return jax.shard_map(
        on_device,
        mesh=mesh,
        in_specs=placed,
        out_specs=P(("grp", "blk", "rep", "sub")),
        check_vma=False,
    )
```

```python
import functools

import jax
import jax.numpy as jnp
from jax import lax
from jax.experimental import pallas as pl
from jax.experimental.pallas import tpu as pltpu
from jax.sharding import PartitionSpec as P

D = 768
GROUPS_EACH_PEER = 3
ORDERS = ((0, 4, 1, 5, 2, 6, 3, 7), (0, 1, 4, 2, 5, 3, 6, 7))
LOADS = 4
MESH = pl.DeviceIdType.MESH
F32 = jnp.float32
BF16 = jnp.bfloat16


def kernel(
    n_blk, n_rep, n_sub, slots,
    x_hbm, label_ref, sizes_ref, heats_ref, out_ref,
    x_ref, unit, out_rows, out_tags, rows, tags, sums, back_out, back_in,
    load_sem, row_send, row_recv, tag_send, tag_recv, fwd_send, fwd_recv,
    fwd_tag_send, fwd_tag_recv, back_send, back_recv,
):
    owners = n_blk * n_rep
    bits = owners.bit_length() - 1
    parts = min(owners, len(ORDERS[0]))
    per = owners // parts
    span = per * slots
    count = x_ref.shape[0]
    me = lax.axis_index("blk") * n_rep + lax.axis_index("rep")
    sub = lax.axis_index("sub")
    sibling = {"sub": 1 - sub}
    piece = count // LOADS

    def load(c):
        at = pl.ds(c * piece, piece)
        return pltpu.make_async_copy(x_hbm.at[at], x_ref.at[at], load_sem.at[c])

    for c in range(LOADS):
        load(c).start()

    def peer(k):
        o = 0
        for b in range(bits):
            o = o + lax.rem(lax.rem(me // 2**b, 2) + lax.rem(k // 2**b, 2), 2) * 2**b
        return o

    def device(owner):
        return {"blk": owner // n_rep, "rep": lax.rem(owner, n_rep)}

    def relative(p):
        near, far = ORDERS[0][p], ORDERS[1][p]
        return near + sub * (far - near)

    def each(p, body):
        def step(q, carry):
            body(p * per + q, peer(relative(p) * per + q))
            return carry

        first = 1 if p == 0 else 0
        if per == 1:
            if not first:
                step(0, 0)
        else:
            lax.fori_loop(first, per, step, 0)

    def peers(body):
        for p in range(parts):
            each(p, body)

    barrier = pltpu.get_barrier_semaphore()
    peers(lambda n, o: pl.semaphore_signal(barrier, inc=1, device_id=device(o), device_id_type=MESH))
    pl.semaphore_signal(barrier, inc=1, device_id=sibling, device_id_type=MESH)

    labels = label_ref[...]
    owner_range = lax.broadcasted_iota(jnp.int32, (owners, count), 0) * GROUPS_EACH_PEER
    local = labels - owner_range
    mine_owner = (local >= 0) & (local < GROUPS_EACH_PEER)
    upper = (
        lax.broadcasted_iota(jnp.int32, (count, count), 0)
        < lax.broadcasted_iota(jnp.int32, (count, count), 1)
    )
    before = jnp.dot(
        jnp.where(mine_owner, 1.0, 0.0).astype(BF16),
        jnp.where(upper, 1.0, 0.0).astype(BF16),
        preferred_element_type=F32,
    )
    rank = jnp.sum(jnp.where(mine_owner, before, 0.0), axis=0, keepdims=True).astype(jnp.int32)
    first = jnp.sum(jnp.where(mine_owner, owner_range, 0), axis=0, keepdims=True)
    member = labels - first
    code = first * 256 + rank
    slot_range = lax.broadcasted_iota(jnp.int32, (slots, count), 0)
    wide_range = lax.broadcasted_iota(jnp.int32, (128, count), 0)
    tag_range = lax.broadcasted_iota(jnp.int32, (8, count), 0)
    tag_table = jnp.where(
        tag_range == GROUPS_EACH_PEER,
        (member + 1).astype(F32),
        jnp.where(tag_range == member, 1.0, 0.0),
    ).astype(BF16)

    def picked(owner, slot):
        return jnp.where(slot + owner * (GROUPS_EACH_PEER * 256) == code, 1.0, 0.0).astype(BF16)

    def tags_for(owner):
        return lax.dot_general(
            tag_table, picked(owner, wide_range), (((1,), (1,)), ((), ())),
            preferred_element_type=F32,
        )

    def rows_for(owner):
        return jnp.dot(
            picked(owner, slot_range), unit[...], preferred_element_type=F32
        ).astype(BF16)

    def normalise(c):
        load(c).wait()
        x = x_ref[c * piece : (c + 1) * piece]
        squares = jnp.sum(x * x, axis=1, keepdims=True)
        unit[c * piece : (c + 1) * piece] = (x * lax.rsqrt(squares + 1e-06)).astype(BF16)

    for c in range(LOADS):
        normalise(c)

    def row_copy(n, o):
        return pltpu.make_async_remote_copy(
            src_ref=out_rows.at[n], dst_ref=rows.at[0, n],
            send_sem=row_send.at[n], recv_sem=row_recv.at[n],
            device_id=device(o), device_id_type=MESH,
        )

    def tag_copy(n, o):
        return pltpu.make_async_remote_copy(
            src_ref=out_tags.at[n], dst_ref=tags.at[0, n],
            send_sem=tag_send.at[n], recv_sem=tag_recv.at[n],
            device_id=device(o), device_id_type=MESH,
        )

    def back_copy(n, o):
        return pltpu.make_async_remote_copy(
            src_ref=back_out.at[n], dst_ref=back_in.at[n],
            send_sem=back_send.at[n], recv_sem=back_recv.at[n],
            device_id=device(o), device_id_type=MESH,
        )

    def forward(n):
        return pltpu.make_async_remote_copy(
            src_ref=rows.at[0, n], dst_ref=rows.at[1, n],
            send_sem=fwd_send.at[n], recv_sem=fwd_recv.at[n],
            device_id=sibling, device_id_type=MESH,
        )

    def send_tags(n, o):
        out_tags[n] = tags_for(o)
        tag_copy(n, o).start()

    def send_rows(n, o):
        out_rows[n] = rows_for(o)
        row_copy(n, o).start()

    starting = [p for p in range(1, parts)] + [0]
    for turn, p in enumerate(starting):
        if turn == 0 and parts > 1:
            def first_rows(n, o):
                out_rows[n] = rows_for(o)

            each(p, first_rows)
            pl.semaphore_wait(barrier, owners)
            each(p, lambda n, o: row_copy(n, o).start())
            peers(send_tags)
            tags[0, 0] = tags_for(me)
        else:
            each(p, send_rows)
    rows[0, 0] = rows_for(me)
    forward(0).start()

    peers(lambda n, o: tag_copy(n, o).wait_recv())
    forward_tags = pltpu.make_async_remote_copy(
        src_ref=tags.at[0], dst_ref=tags.at[1],
        send_sem=fwd_tag_send, recv_sem=fwd_tag_recv,
        device_id=sibling, device_id_type=MESH,
    )
    forward_tags.start()

    hot = jnp.concatenate([tags[0, n][:, :slots] for n in range(owners)], axis=1)
    heat = jnp.zeros_like(hot[0:1])
    size = jnp.zeros_like(heat)
    for g in range(GROUPS_EACH_PEER):
        at = me * GROUPS_EACH_PEER + g
        heat = heat + hot[g : g + 1] * heats_ref[at]
        size = jnp.where(hot[g : g + 1] > 0.5, sizes_ref[at].astype(F32), size)
    valid = heat > 0.0
    inverse = 1.0 / jnp.where(valid, heat, 1.0)
    offset = inverse - jnp.log(jnp.where(valid, size, 1.0))
    tag_row = hot[GROUPS_EACH_PEER : GROUPS_EACH_PEER + 1]
    forward_tags.wait_recv()

    def tag_column(s, lo, hi):
        return jnp.concatenate(
            [
                tags[s, n].T[:slots, GROUPS_EACH_PEER : GROUPS_EACH_PEER + 1]
                for n in range(lo * per, hi * per)
            ],
            axis=0,
        )

    def block(s, lo, hi):
        return rows[s, lo * per : hi * per].reshape((hi - lo) * span, D)

    def column(s, j0, j1, i0, i1):
        cosine = lax.dot_general(
            block(s, j0, j1), block(0, i0, i1), (((1,), (1,)), ((), ())),
            preferred_element_type=F32,
        )
        at = slice(i0 * span, i1 * span)
        weight = jnp.where(
            tag_column(s, j0, j1) == tag_row[:, at],
            jnp.exp((cosine - 1.0) * inverse[:, at]),
            0.0,
        )
        return jnp.sum(weight, axis=0, keepdims=True)

    def arrive_sibling(p):
        if p == 0:
            forward(0).wait_recv()
        each(p, lambda n, o: forward(n).wait_recv())

    def arrive(n, o):
        row_copy(n, o).wait_recv()
        forward(n).start()

    sums[...] = jnp.zeros_like(sums)
    back_out[...] = jnp.zeros_like(back_out)
    late = []
    for p in range(parts):
        each(p, arrive)
        upto = slice(0, (p + 1) * span)
        part = column(0, p, p + 1, 0, p + 1)
        extra = jnp.zeros((1, span), F32)
        if p:
            extra = extra + column(0, 0, p, p, p + 1)
            if p > 1:
                extra = extra + column(1, 0, p - 1, p, p + 1)
            arrive_sibling(p - 1)
            part = part + column(1, p - 1, p, 0, p + 1)
        late.append(extra)
        sums[:, upto] += part
    arrive_sibling(parts - 1)
    sums[...] += column(1, parts - 1, parts, 0, parts)

    total = sums[...] + jnp.concatenate(late, axis=1)
    scores = jnp.where(valid, offset + jnp.log(jnp.where(valid, total, 1.0)), 0.0)
    for n in range(owners):
        back_out[n, 0:1, 0:slots] = scores[:, n * slots : (n + 1) * slots]
    peers(lambda n, o: back_copy(n, o).start())
    back_in[0] = back_out[0]

    def drain(n, o):
        tag_copy(n, o).wait_send()
        row_copy(n, o).wait_send()
        forward(n).wait_send()

    peers(drain)
    forward(0).wait_send()
    forward_tags.wait_send()
    spread = jnp.where(wide_range == rank, 1.0, 0.0)

    peers(lambda n, o: back_copy(n, o).wait_recv())
    table = back_in[:, 0, :]
    found = jnp.dot(table, spread, precision=lax.Precision.HIGHEST, preferred_element_type=F32)
    out = jnp.where(first == me * GROUPS_EACH_PEER, found[0:1], 0.0)
    for n in range(1, owners):
        o = peer(relative(n // per) * per + n % per)
        out = jnp.where(first == o * GROUPS_EACH_PEER, found[n : n + 1], out)
    out_ref[...] = out
    peers(lambda n, o: back_copy(n, o).wait_send())


def on_device(vectors, labels, sizes, heats):
    count = vectors.shape[0]
    n_blk, n_rep, n_sub = (lax.axis_size(a) for a in ("blk", "rep", "sub"))
    owners = n_blk * n_rep
    share = count // owners
    slots = -(-(share + share // 2) // 16) * 16
    dma = pltpu.SemaphoreType.DMA
    out = pl.pallas_call(
        functools.partial(kernel, n_blk, n_rep, n_sub, slots),
        out_shape=jax.ShapeDtypeStruct((1, count), F32),
        in_specs=[
            pl.BlockSpec(memory_space=pltpu.HBM),
            pl.BlockSpec(memory_space=pltpu.VMEM),
            pl.BlockSpec(memory_space=pltpu.SMEM),
            pl.BlockSpec(memory_space=pltpu.SMEM),
        ],
        out_specs=pl.BlockSpec(memory_space=pltpu.VMEM),
        scratch_shapes=[
            pltpu.VMEM((count, D), F32),
            pltpu.VMEM((count, D), BF16),
            pltpu.VMEM((owners, slots, D), BF16),
            pltpu.VMEM((owners, 8, 128), F32),
            pltpu.VMEM((n_sub, owners, slots, D), BF16),
            pltpu.VMEM((n_sub, owners, 8, 128), F32),
            pltpu.VMEM((1, owners * slots), F32),
            pltpu.VMEM((owners, 8, 128), F32),
            pltpu.VMEM((owners, 8, 128), F32),
            dma((LOADS,)),
            dma((owners,)), dma((owners,)), dma((owners,)), dma((owners,)),
            dma((owners,)), dma((owners,)), dma, dma,
            dma((owners,)), dma((owners,)),
        ],
        compiler_params=pltpu.CompilerParams(
            collective_id=0, has_side_effects=True, vmem_limit_bytes=48 << 20
        ),
    )(vectors, labels.reshape(1, count), sizes, heats)
    return out.reshape(count)


def solution(mesh):
    placed = (
        P(("grp", "blk", "rep", "sub"), None),
        P(("grp", "blk", "rep", "sub")),
        P("grp"),
        P("grp"),
    )
    return jax.shard_map(
        on_device,
        mesh=mesh,
        in_specs=placed,
        out_specs=P(("grp", "blk", "rep", "sub")),
        check_vma=False,
    )
```

```python
import functools

import jax
import jax.numpy as jnp
from jax import lax
from jax.experimental import pallas as pl
from jax.experimental.pallas import tpu as pltpu
from jax.sharding import PartitionSpec as P

D = 768
GROUPS_EACH_PEER = 3
ORDERS = ((0, 4, 1, 5, 2, 6, 3, 7), (0, 1, 4, 2, 5, 3, 6, 7))
LOADS = 4
MESH = pl.DeviceIdType.MESH
F32 = jnp.float32
BF16 = jnp.bfloat16


def kernel(
    n_blk, n_rep, n_sub, slots,
    x_hbm, label_ref, sizes_ref, heats_ref, out_ref,
    x_ref, unit, out_rows, out_tags, rows, tags, sums, back_out, back_in,
    load_sem, row_send, row_recv, tag_send, tag_recv, fwd_send, fwd_recv,
    fwd_tag_send, fwd_tag_recv, back_send, back_recv,
):
    owners = n_blk * n_rep
    bits = owners.bit_length() - 1
    parts = min(owners, len(ORDERS[0]))
    per = owners // parts
    span = per * slots
    count = x_ref.shape[0]
    me = lax.axis_index("blk") * n_rep + lax.axis_index("rep")
    sub = lax.axis_index("sub")
    sibling = {"sub": 1 - sub}
    piece = count // LOADS

    def load(c):
        at = pl.ds(c * piece, piece)
        return pltpu.make_async_copy(x_hbm.at[at], x_ref.at[at], load_sem.at[c])

    for c in range(LOADS):
        load(c).start()

    def peer(k):
        o = 0
        for b in range(bits):
            o = o + lax.rem(lax.rem(me // 2**b, 2) + lax.rem(k // 2**b, 2), 2) * 2**b
        return o

    def device(owner):
        return {"blk": owner // n_rep, "rep": lax.rem(owner, n_rep)}

    def relative(p):
        near, far = ORDERS[0][p], ORDERS[1][p]
        return near + sub * (far - near)

    def each(p, body):
        def step(q, carry):
            body(p * per + q, peer(relative(p) * per + q))
            return carry

        first = 1 if p == 0 else 0
        if per == 1:
            if not first:
                step(0, 0)
        else:
            lax.fori_loop(first, per, step, 0)

    def peers(body):
        for p in range(parts):
            each(p, body)

    barrier = pltpu.get_barrier_semaphore()
    peers(lambda n, o: pl.semaphore_signal(barrier, inc=1, device_id=device(o), device_id_type=MESH))
    pl.semaphore_signal(barrier, inc=1, device_id=sibling, device_id_type=MESH)

    labels = label_ref[...]
    owner_range = lax.broadcasted_iota(jnp.int32, (owners, count), 0) * GROUPS_EACH_PEER
    local = labels - owner_range
    mine_owner = (local >= 0) & (local < GROUPS_EACH_PEER)
    upper = (
        lax.broadcasted_iota(jnp.int32, (count, count), 0)
        < lax.broadcasted_iota(jnp.int32, (count, count), 1)
    )
    before = jnp.dot(
        jnp.where(mine_owner, 1.0, 0.0).astype(BF16),
        jnp.where(upper, 1.0, 0.0).astype(BF16),
        preferred_element_type=F32,
    )
    rank = jnp.sum(jnp.where(mine_owner, before, 0.0), axis=0, keepdims=True).astype(jnp.int32)
    first = jnp.sum(jnp.where(mine_owner, owner_range, 0), axis=0, keepdims=True)
    member = labels - first
    code = first * 256 + rank
    slot_range = lax.broadcasted_iota(jnp.int32, (slots, count), 0)
    wide_range = lax.broadcasted_iota(jnp.int32, (128, count), 0)
    tag_range = lax.broadcasted_iota(jnp.int32, (8, count), 0)
    tag_table = jnp.where(
        tag_range == GROUPS_EACH_PEER,
        (member + 1).astype(F32),
        jnp.where(tag_range == member, 1.0, 0.0),
    ).astype(BF16)

    def picked(owner, slot):
        return jnp.where(slot + owner * (GROUPS_EACH_PEER * 256) == code, 1.0, 0.0).astype(BF16)

    def tags_for(owner):
        return lax.dot_general(
            tag_table, picked(owner, wide_range), (((1,), (1,)), ((), ())),
            preferred_element_type=F32,
        )

    def rows_for(owner):
        return jnp.dot(
            picked(owner, slot_range), unit[...], preferred_element_type=F32
        ).astype(BF16)

    def normalise(c):
        load(c).wait()
        x = x_ref[c * piece : (c + 1) * piece]
        squares = jnp.sum(x * x, axis=1, keepdims=True)
        unit[c * piece : (c + 1) * piece] = (x * lax.rsqrt(squares + 1e-06)).astype(BF16)

    for c in range(LOADS):
        normalise(c)

    def row_copy(n, o):
        return pltpu.make_async_remote_copy(
            src_ref=out_rows.at[n], dst_ref=rows.at[0, n],
            send_sem=row_send.at[n], recv_sem=row_recv.at[n],
            device_id=device(o), device_id_type=MESH,
        )

    def tag_copy(n, o):
        return pltpu.make_async_remote_copy(
            src_ref=out_tags.at[n], dst_ref=tags.at[0, n],
            send_sem=tag_send.at[n], recv_sem=tag_recv.at[n],
            device_id=device(o), device_id_type=MESH,
        )

    def back_copy(n, o):
        return pltpu.make_async_remote_copy(
            src_ref=back_out.at[n], dst_ref=back_in.at[n],
            send_sem=back_send.at[n], recv_sem=back_recv.at[n],
            device_id=device(o), device_id_type=MESH,
        )

    def forward(n):
        return pltpu.make_async_remote_copy(
            src_ref=rows.at[0, n], dst_ref=rows.at[1, n],
            send_sem=fwd_send.at[n], recv_sem=fwd_recv.at[n],
            device_id=sibling, device_id_type=MESH,
        )

    def send_tags(n, o):
        out_tags[n] = tags_for(o)
        tag_copy(n, o).start()

    def send_rows(n, o):
        out_rows[n] = rows_for(o)
        row_copy(n, o).start()

    starting = [p for p in range(1, parts)] + [0]
    for turn, p in enumerate(starting):
        if turn == 0 and parts > 1:
            def first_rows(n, o):
                out_rows[n] = rows_for(o)

            each(p, first_rows)
            pl.semaphore_wait(barrier, owners)
            each(p, lambda n, o: row_copy(n, o).start())
        else:
            each(p, send_rows)
        if turn == min(1, parts - 2):
            peers(send_tags)
            tags[0, 0] = tags_for(me)
    rows[0, 0] = rows_for(me)
    forward(0).start()

    peers(lambda n, o: tag_copy(n, o).wait_recv())
    forward_tags = pltpu.make_async_remote_copy(
        src_ref=tags.at[0], dst_ref=tags.at[1],
        send_sem=fwd_tag_send, recv_sem=fwd_tag_recv,
        device_id=sibling, device_id_type=MESH,
    )
    forward_tags.start()

    hot = jnp.concatenate([tags[0, n][:, :slots] for n in range(owners)], axis=1)
    heat = jnp.zeros_like(hot[0:1])
    size = jnp.zeros_like(heat)
    for g in range(GROUPS_EACH_PEER):
        at = me * GROUPS_EACH_PEER + g
        heat = heat + hot[g : g + 1] * heats_ref[at]
        size = jnp.where(hot[g : g + 1] > 0.5, sizes_ref[at].astype(F32), size)
    valid = heat > 0.0
    inverse = 1.0 / jnp.where(valid, heat, 1.0)
    offset = inverse - jnp.log(jnp.where(valid, size, 1.0))
    tag_row = hot[GROUPS_EACH_PEER : GROUPS_EACH_PEER + 1]
    forward_tags.wait_recv()

    def tag_column(s, lo, hi):
        return jnp.concatenate(
            [
                tags[s, n].T[:slots, GROUPS_EACH_PEER : GROUPS_EACH_PEER + 1]
                for n in range(lo * per, hi * per)
            ],
            axis=0,
        )

    def block(s, lo, hi):
        return rows[s, lo * per : hi * per].reshape((hi - lo) * span, D)

    def column(s, j0, j1, i0, i1):
        cosine = lax.dot_general(
            block(s, j0, j1), block(0, i0, i1), (((1,), (1,)), ((), ())),
            preferred_element_type=F32,
        )
        at = slice(i0 * span, i1 * span)
        weight = jnp.where(
            tag_column(s, j0, j1) == tag_row[:, at],
            jnp.exp((cosine - 1.0) * inverse[:, at]),
            0.0,
        )
        return jnp.sum(weight, axis=0, keepdims=True)

    def arrive_sibling(p):
        if p == 0:
            forward(0).wait_recv()
        each(p, lambda n, o: forward(n).wait_recv())

    def arrive(n, o):
        row_copy(n, o).wait_recv()
        forward(n).start()

    sums[...] = jnp.zeros_like(sums)
    back_out[...] = jnp.zeros_like(back_out)
    late = []
    step = -(-parts // 4)
    for lo in range(0, parts, step):
        hi = lo + step
        for p in range(lo, hi):
            each(p, arrive)
        part = column(0, lo, hi, 0, hi)
        extra = jnp.zeros((1, (hi - lo) * span), F32)
        if lo:
            extra = column(0, 0, lo, lo, hi) + column(1, 0, lo, lo, hi)
        late.append(extra)
        for p in range(lo, hi):
            arrive_sibling(p)
        sums[:, 0 : hi * span] += part + column(1, lo, hi, 0, hi)

    total = sums[...] + jnp.concatenate(late, axis=1)
    scores = jnp.where(valid, offset + jnp.log(jnp.where(valid, total, 1.0)), 0.0)
    for n in range(owners):
        back_out[n, 0:1, 0:slots] = scores[:, n * slots : (n + 1) * slots]
    peers(lambda n, o: back_copy(n, o).start())
    back_in[0] = back_out[0]

    def drain(n, o):
        tag_copy(n, o).wait_send()
        row_copy(n, o).wait_send()
        forward(n).wait_send()

    peers(drain)
    forward(0).wait_send()
    forward_tags.wait_send()
    spread = jnp.where(wide_range == rank, 1.0, 0.0)

    peers(lambda n, o: back_copy(n, o).wait_recv())
    table = back_in[:, 0, :]
    found = jnp.dot(table, spread, precision=lax.Precision.HIGHEST, preferred_element_type=F32)
    out = jnp.where(first == me * GROUPS_EACH_PEER, found[0:1], 0.0)
    for n in range(1, owners):
        o = peer(relative(n // per) * per + n % per)
        out = jnp.where(first == o * GROUPS_EACH_PEER, found[n : n + 1], out)
    out_ref[...] = out
    peers(lambda n, o: back_copy(n, o).wait_send())


def on_device(vectors, labels, sizes, heats):
    count = vectors.shape[0]
    n_blk, n_rep, n_sub = (lax.axis_size(a) for a in ("blk", "rep", "sub"))
    owners = n_blk * n_rep
    share = count // owners
    slots = -(-(share + share // 2) // 16) * 16
    dma = pltpu.SemaphoreType.DMA
    out = pl.pallas_call(
        functools.partial(kernel, n_blk, n_rep, n_sub, slots),
        out_shape=jax.ShapeDtypeStruct((1, count), F32),
        in_specs=[
            pl.BlockSpec(memory_space=pltpu.HBM),
            pl.BlockSpec(memory_space=pltpu.VMEM),
            pl.BlockSpec(memory_space=pltpu.SMEM),
            pl.BlockSpec(memory_space=pltpu.SMEM),
        ],
        out_specs=pl.BlockSpec(memory_space=pltpu.VMEM),
        scratch_shapes=[
            pltpu.VMEM((count, D), F32),
            pltpu.VMEM((count, D), BF16),
            pltpu.VMEM((owners, slots, D), BF16),
            pltpu.VMEM((owners, 8, 128), F32),
            pltpu.VMEM((n_sub, owners, slots, D), BF16),
            pltpu.VMEM((n_sub, owners, 8, 128), F32),
            pltpu.VMEM((1, owners * slots), F32),
            pltpu.VMEM((owners, 8, 128), F32),
            pltpu.VMEM((owners, 8, 128), F32),
            dma((LOADS,)),
            dma((owners,)), dma((owners,)), dma((owners,)), dma((owners,)),
            dma((owners,)), dma((owners,)), dma, dma,
            dma((owners,)), dma((owners,)),
        ],
        compiler_params=pltpu.CompilerParams(
            collective_id=0, has_side_effects=True, vmem_limit_bytes=64 << 20
        ),
    )(vectors, labels.reshape(1, count), sizes, heats)
    return out.reshape(count)


def solution(mesh):
    placed = (
        P(("grp", "blk", "rep", "sub"), None),
        P(("grp", "blk", "rep", "sub")),
        P("grp"),
        P("grp"),
    )
    return jax.shard_map(
        on_device,
        mesh=mesh,
        in_specs=placed,
        out_specs=P(("grp", "blk", "rep", "sub")),
        check_vma=False,
    )
```

```python
import functools

import jax
import jax.numpy as jnp
from jax import lax
from jax.experimental import pallas as pl
from jax.experimental.pallas import tpu as pltpu
from jax.sharding import PartitionSpec as P

D = 768
GROUPS_EACH_PEER = 3
ORDERS = ((0, 4, 1, 5, 2, 6, 3, 7), (0, 1, 4, 2, 5, 3, 6, 7))
LOADS = 4
MESH = pl.DeviceIdType.MESH
F32 = jnp.float32
BF16 = jnp.bfloat16


def kernel(
    n_blk, n_rep, n_sub, slots,
    x_hbm, label_ref, sizes_ref, heats_ref, out_ref,
    x_ref, unit, out_rows, out_tags, rows, tags, sums, back_out, back_in,
    load_sem, row_send, row_recv, tag_send, tag_recv, fwd_send, fwd_recv,
    fwd_tag_send, fwd_tag_recv, back_send, back_recv,
):
    owners = n_blk * n_rep
    bits = owners.bit_length() - 1
    parts = min(owners, len(ORDERS[0]))
    per = owners // parts
    span = per * slots
    count = x_ref.shape[0]
    me = lax.axis_index("blk") * n_rep + lax.axis_index("rep")
    sub = lax.axis_index("sub")
    sibling = {"sub": 1 - sub}
    piece = count // LOADS

    def load(c):
        at = pl.ds(c * piece, piece)
        return pltpu.make_async_copy(x_hbm.at[at], x_ref.at[at], load_sem.at[c])

    for c in range(LOADS):
        load(c).start()

    def peer(k):
        o = 0
        for b in range(bits):
            o = o + lax.rem(lax.rem(me // 2**b, 2) + lax.rem(k // 2**b, 2), 2) * 2**b
        return o

    def device(owner):
        return {"blk": owner // n_rep, "rep": lax.rem(owner, n_rep)}

    def relative(p):
        near, far = ORDERS[0][p], ORDERS[1][p]
        return near + sub * (far - near)

    def each(p, body):
        def step(q, carry):
            body(p * per + q, peer(relative(p) * per + q))
            return carry

        first = 1 if p == 0 else 0
        if per == 1:
            if not first:
                step(0, 0)
        else:
            lax.fori_loop(first, per, step, 0)

    def peers(body):
        for p in range(parts):
            each(p, body)

    barrier = pltpu.get_barrier_semaphore()
    peers(lambda n, o: pl.semaphore_signal(barrier, inc=1, device_id=device(o), device_id_type=MESH))
    pl.semaphore_signal(barrier, inc=1, device_id=sibling, device_id_type=MESH)

    labels = label_ref[...]
    owner_range = lax.broadcasted_iota(jnp.int32, (owners, count), 0) * GROUPS_EACH_PEER
    local = labels - owner_range
    mine_owner = (local >= 0) & (local < GROUPS_EACH_PEER)
    upper = (
        lax.broadcasted_iota(jnp.int32, (count, count), 0)
        < lax.broadcasted_iota(jnp.int32, (count, count), 1)
    )
    before = jnp.dot(
        jnp.where(mine_owner, 1.0, 0.0).astype(BF16),
        jnp.where(upper, 1.0, 0.0).astype(BF16),
        preferred_element_type=F32,
    )
    rank = jnp.sum(jnp.where(mine_owner, before, 0.0), axis=0, keepdims=True).astype(jnp.int32)
    first = jnp.sum(jnp.where(mine_owner, owner_range, 0), axis=0, keepdims=True)
    member = labels - first
    code = first * 256 + rank
    slot_range = lax.broadcasted_iota(jnp.int32, (slots, count), 0)
    wide_range = lax.broadcasted_iota(jnp.int32, (128, count), 0)
    tag_range = lax.broadcasted_iota(jnp.int32, (8, count), 0)
    tag_table = jnp.where(
        tag_range == GROUPS_EACH_PEER,
        (member + 1).astype(F32),
        jnp.where(tag_range == member, 1.0, 0.0),
    ).astype(BF16)

    def picked(owner, slot):
        return jnp.where(slot + owner * (GROUPS_EACH_PEER * 256) == code, 1.0, 0.0).astype(BF16)

    def tags_for(owner):
        return lax.dot_general(
            tag_table, picked(owner, wide_range), (((1,), (1,)), ((), ())),
            preferred_element_type=F32,
        )

    def rows_for(owner):
        return jnp.dot(
            picked(owner, slot_range), unit[...], preferred_element_type=F32
        ).astype(BF16)

    def normalise(c):
        load(c).wait()
        x = x_ref[c * piece : (c + 1) * piece]
        squares = jnp.sum(x * x, axis=1, keepdims=True)
        unit[c * piece : (c + 1) * piece] = (x * lax.rsqrt(squares + 1e-06)).astype(BF16)

    def make_tags(n, o):
        out_tags[n] = tags_for(o)

    peers(make_tags)
    tags[0, 0] = tags_for(me)
    for c in range(LOADS):
        normalise(c)

    def row_copy(n, o):
        return pltpu.make_async_remote_copy(
            src_ref=out_rows.at[n], dst_ref=rows.at[0, n],
            send_sem=row_send.at[n], recv_sem=row_recv.at[n],
            device_id=device(o), device_id_type=MESH,
        )

    def tag_copy(n, o):
        return pltpu.make_async_remote_copy(
            src_ref=out_tags.at[n], dst_ref=tags.at[0, n],
            send_sem=tag_send.at[n], recv_sem=tag_recv.at[n],
            device_id=device(o), device_id_type=MESH,
        )

    def back_copy(n, o):
        return pltpu.make_async_remote_copy(
            src_ref=back_out.at[n], dst_ref=back_in.at[n],
            send_sem=back_send.at[n], recv_sem=back_recv.at[n],
            device_id=device(o), device_id_type=MESH,
        )

    def forward(n):
        return pltpu.make_async_remote_copy(
            src_ref=rows.at[0, n], dst_ref=rows.at[1, n],
            send_sem=fwd_send.at[n], recv_sem=fwd_recv.at[n],
            device_id=sibling, device_id_type=MESH,
        )

    def send_rows(n, o):
        out_rows[n] = rows_for(o)
        row_copy(n, o).start()

    starting = [p for p in range(1, parts)] + [0]
    for turn, p in enumerate(starting):
        if turn == 0 and parts > 1:
            def first_rows(n, o):
                out_rows[n] = rows_for(o)

            each(p, first_rows)
            pl.semaphore_wait(barrier, owners)
            peers(lambda n, o: tag_copy(n, o).start())
            each(p, lambda n, o: row_copy(n, o).start())
        else:
            each(p, send_rows)
    rows[0, 0] = rows_for(me)
    forward(0).start()

    peers(lambda n, o: tag_copy(n, o).wait_recv())
    forward_tags = pltpu.make_async_remote_copy(
        src_ref=tags.at[0], dst_ref=tags.at[1],
        send_sem=fwd_tag_send, recv_sem=fwd_tag_recv,
        device_id=sibling, device_id_type=MESH,
    )
    forward_tags.start()

    hot = jnp.concatenate([tags[0, n][:, :slots] for n in range(owners)], axis=1)
    heat = jnp.zeros_like(hot[0:1])
    size = jnp.zeros_like(heat)
    for g in range(GROUPS_EACH_PEER):
        at = me * GROUPS_EACH_PEER + g
        heat = heat + hot[g : g + 1] * heats_ref[at]
        size = jnp.where(hot[g : g + 1] > 0.5, sizes_ref[at].astype(F32), size)
    valid = heat > 0.0
    inverse = 1.0 / jnp.where(valid, heat, 1.0)
    offset = inverse - jnp.log(jnp.where(valid, size, 1.0))
    tag_row = hot[GROUPS_EACH_PEER : GROUPS_EACH_PEER + 1]
    forward_tags.wait_recv()

    def tag_column(s, lo, hi):
        return jnp.concatenate(
            [
                tags[s, n].T[:slots, GROUPS_EACH_PEER : GROUPS_EACH_PEER + 1]
                for n in range(lo * per, hi * per)
            ],
            axis=0,
        )

    def block(s, lo, hi):
        return rows[s, lo * per : hi * per].reshape((hi - lo) * span, D)

    def column(s, j0, j1, i0, i1):
        cosine = lax.dot_general(
            block(s, j0, j1), block(0, i0, i1), (((1,), (1,)), ((), ())),
            preferred_element_type=F32,
        )
        at = slice(i0 * span, i1 * span)
        weight = jnp.where(
            tag_column(s, j0, j1) == tag_row[:, at],
            jnp.exp((cosine - 1.0) * inverse[:, at]),
            0.0,
        )
        return jnp.sum(weight, axis=0, keepdims=True)

    def arrive_sibling(p):
        if p == 0:
            forward(0).wait_recv()
        each(p, lambda n, o: forward(n).wait_recv())

    def arrive(n, o):
        row_copy(n, o).wait_recv()
        forward(n).start()

    sums[...] = jnp.zeros_like(sums)
    back_out[...] = jnp.zeros_like(back_out)
    late = []
    step = -(-parts // 4)
    for lo in range(0, parts, step):
        hi = lo + step
        for p in range(lo, hi):
            each(p, arrive)
        part = column(0, lo, hi, 0, hi)
        extra = jnp.zeros((1, (hi - lo) * span), F32)
        if lo:
            extra = column(0, 0, lo, lo, hi) + column(1, 0, lo, lo, hi)
        late.append(extra)
        for p in range(lo, hi):
            arrive_sibling(p)
        sums[:, 0 : hi * span] += part + column(1, lo, hi, 0, hi)

    total = sums[...] + jnp.concatenate(late, axis=1)
    scores = jnp.where(valid, offset + jnp.log(jnp.where(valid, total, 1.0)), 0.0)
    for n in range(owners):
        back_out[n, 0:1, 0:slots] = scores[:, n * slots : (n + 1) * slots]
    peers(lambda n, o: back_copy(n, o).start())
    back_in[0] = back_out[0]

    def drain(n, o):
        tag_copy(n, o).wait_send()
        row_copy(n, o).wait_send()
        forward(n).wait_send()

    peers(drain)
    forward(0).wait_send()
    forward_tags.wait_send()
    spread = jnp.where(wide_range == rank, 1.0, 0.0)

    peers(lambda n, o: back_copy(n, o).wait_recv())
    table = back_in[:, 0, :]
    found = jnp.dot(table, spread, precision=lax.Precision.HIGHEST, preferred_element_type=F32)
    out = jnp.where(first == me * GROUPS_EACH_PEER, found[0:1], 0.0)
    for n in range(1, owners):
        o = peer(relative(n // per) * per + n % per)
        out = jnp.where(first == o * GROUPS_EACH_PEER, found[n : n + 1], out)
    out_ref[...] = out
    peers(lambda n, o: back_copy(n, o).wait_send())


def on_device(vectors, labels, sizes, heats):
    count = vectors.shape[0]
    n_blk, n_rep, n_sub = (lax.axis_size(a) for a in ("blk", "rep", "sub"))
    owners = n_blk * n_rep
    share = count // owners
    slots = -(-(share + share // 2) // 16) * 16
    dma = pltpu.SemaphoreType.DMA
    out = pl.pallas_call(
        functools.partial(kernel, n_blk, n_rep, n_sub, slots),
        out_shape=jax.ShapeDtypeStruct((1, count), F32),
        in_specs=[
            pl.BlockSpec(memory_space=pltpu.HBM),
            pl.BlockSpec(memory_space=pltpu.VMEM),
            pl.BlockSpec(memory_space=pltpu.SMEM),
            pl.BlockSpec(memory_space=pltpu.SMEM),
        ],
        out_specs=pl.BlockSpec(memory_space=pltpu.VMEM),
        scratch_shapes=[
            pltpu.VMEM((count, D), F32),
            pltpu.VMEM((count, D), BF16),
            pltpu.VMEM((owners, slots, D), BF16),
            pltpu.VMEM((owners, 8, 128), F32),
            pltpu.VMEM((n_sub, owners, slots, D), BF16),
            pltpu.VMEM((n_sub, owners, 8, 128), F32),
            pltpu.VMEM((1, owners * slots), F32),
            pltpu.VMEM((owners, 8, 128), F32),
            pltpu.VMEM((owners, 8, 128), F32),
            dma((LOADS,)),
            dma((owners,)), dma((owners,)), dma((owners,)), dma((owners,)),
            dma((owners,)), dma((owners,)), dma, dma,
            dma((owners,)), dma((owners,)),
        ],
        compiler_params=pltpu.CompilerParams(
            collective_id=0, has_side_effects=True, vmem_limit_bytes=64 << 20
        ),
    )(vectors, labels.reshape(1, count), sizes, heats)
    return out.reshape(count)


def solution(mesh):
    placed = (
        P(("grp", "blk", "rep", "sub"), None),
        P(("grp", "blk", "rep", "sub")),
        P("grp"),
        P("grp"),
    )
    return jax.shard_map(
        on_device,
        mesh=mesh,
        in_specs=placed,
        out_specs=P(("grp", "blk", "rep", "sub")),
        check_vma=False,
    )
```
